128 devices in a mesh: group: 2 (over z_hi), ctx: 8 (over z_lo, x), tp: 8 (over y, core).
Axes of the slice: x: 4, y: 4, z: 4 (z_hi: 2, z_lo: 2; z = z_hi * 2 + z_lo), core: 2. Of those that a mesh axis runs over, the one named last changes fastest.
Arguments:
- hidden_in: bfloat16 [2, 512, 16384], P('group', None, 'ctx'), may hold values from -6 to 6
- w_query: bfloat16 [16384, 8192], P('ctx', 'tp'), may hold values from -0.046875 to 0.046875
- w_keyval: bfloat16 [16384, 2048], P('ctx', 'tp'), may hold values from -0.046875 to 0.046875
- w_out: bfloat16 [8192, 16384], P('tp', 'ctx'), may hold values from -0.0625 to 0.0625
- kv_pages: bfloat16 [2, 512, 64, 2048], P('group', 'ctx', None, 'tp'), may hold values from -500 to 500
- page_slot: int32 [512], replicated, may hold values from 0 to 511, as said below
- lengths: int32 [512], P('ctx'), may hold values from 1 to 64, 16384 in all
Outputs:
- attn_out: bfloat16 [2, 512, 16384], P('group', 'tp', 'ctx')
- page_pools: bfloat16 [2, 512, 64, 2048], P('group', 'ctx', None, 'tp')
The draws below stay inside these ranges and needn't reach their ends.
Inputs may be any that keep to these rules, and one draw needn't show every extreme that they name: page_slot is a permutation of the 512 pool slots; each aligned block of 64 pages sends exactly 8 pages into each aligned block of 64 slots. `lengths`: positions of a decode row at or beyond its length are not part of its context.
All inputs are finite; a program needn't handle non-finite values. No bound on the sum of `lengths` on one device may be relied on, other than what follows from the above.
Results may differ from the reference program's by a relative error of at most 0.019.
The reference program's roundings to bfloat16 on the way count: a program that leaves them out, or rounds other values in their place, can miss the bound.
Values may be sent and summed in bfloat16 or wider, within the bound.
No kernel may reach another device: no remote copies, remote signals or barrier semaphores. Data moves between devices by JAX's collectives and lax.ppermute only.
A program may use at most 128 MiB of HBM per device.

```python
import math
import jax
import jax.numpy as jnp
import numpy as np
from jax import lax

D = 16384
KVH = 8
HD = 128
HQ = 64
PAGE = 64
PAGES_DEV = 64
ROWS = 512
PAGES = 512
DEPTH = 32768
RES = 64
GROUP_Q = 8
N_CTX = 8
N_TP = 8


def draw_kv_pages(key, part):
    key = jax.random.fold_in(key, 11)
    k_base = jax.random.fold_in(key, 0)
    full_shape = (2, PAGES, PAGE, KVH, 2, HD)
    stacked = jnp.clip(jax.random.normal(k_base, full_shape, jnp.float32), -4.0, 4.0)
    return stacked.reshape(2, PAGES, PAGE, KVH * 2 * HD).astype(jnp.bfloat16)


def permute_pages(sub_key):
    return jax.random.permutation(sub_key, PAGES_DEV)


def draw_page_slot(key, part):
    key = jax.random.fold_in(key, 5)
    k_send, k_place = jax.random.split(key)
    blocks = PAGES // PAGES_DEV
    per_peer = PAGES_DEV // blocks
    send_perm = jax.vmap(permute_pages)(jax.random.split(k_send, blocks))
    place_perm = jax.vmap(permute_pages)(jax.random.split(k_place, blocks))
    target = send_perm // per_peer
    arrival = jnp.arange(blocks, dtype=jnp.int32)[:, None] * per_peer + send_perm % per_peer
    local_slot = place_perm[target, arrival]
    return (target * PAGES_DEV + local_slot).reshape(PAGES).astype(jnp.int32)


def level_of(key, shape, cuts, low, high):
    def one(axis_at, shards_of):
        steps = jax.random.uniform(jax.random.fold_in(jax.random.fold_in(key, 6), axis_at), (shards_of,), jnp.float32, low / len(cuts), high / len(cuts))
        return jnp.repeat(jnp.exp(steps), shape[axis_at] // shards_of).reshape((-1,) + (1,) * (len(shape) - axis_at - 1))

    factor_of = one(*cuts[0])
    for cut in cuts[1:]:
        factor_of = factor_of * one(*cut)
    return factor_of


def split_up(count, total, limit, slope):
    portions = [(1 << 20) // math.isqrt(standing ** slope) + 1 for standing in range(2, count + 1)]
    rest, counts = total - limit - (count - 1), [1] * (count - 1)
    while rest > 0:
        candidates = [i for i in range(count - 1) if counts[i] < limit]
        whole, remaining = sum([portions[i] for i in candidates]), rest
        for i in candidates:
            more = min(limit - counts[i], max(1, remaining * portions[i] // whole), rest)
            counts[i] = counts[i] + more
            rest = rest - more
    return np.array([limit] + counts)


def ragged_sizes(own_key, count, total, most, slope):
    if count == 2:
        one = jax.random.randint(own_key, (), max(1, total - most), min(most, total - 1) + 1)
        return jnp.stack([one, total - one])
    sizes = jnp.asarray(split_up(count, total, most, slope), jnp.int32)
    twos = (count - 1) // 2
    giver, sink = sizes[1:1 + 2 * twos:2], sizes[2:2 + 2 * twos:2]
    slack = jnp.minimum(giver - 1, most - sink)
    moved = jax.random.randint(jax.random.fold_in(own_key, 1), (twos,), 0, 1 << 20) % (slack + 1)
    sizes = sizes.at[1:1 + 2 * twos:2].set(giver - moved).at[2:2 + 2 * twos:2].set(sink + moved)
    return sizes[jax.random.permutation(jax.random.fold_in(own_key, 2), count)]


def normal_values(rng, shape, width, reach, cuts=(), kind=jnp.bfloat16):
    loudness = level_of(rng, shape, cuts, -0.22, 0.18) if cuts else 1.0
    entries = jax.random.normal(rng, shape, jnp.float32) * width * loudness
    return jnp.minimum(jnp.maximum(entries, -reach), reach).astype(kind)


def setup_inputs(seed: int = 0) -> dict:
    streams_of = jax.random.split(jax.random.key(seed), 8)
    return {
        "hidden_in": normal_values(streams_of[0], (2, ROWS, D), 1.0, 6.0, ((0, 2), (2, 8))),
        "w_query": normal_values(streams_of[1], (D, HQ * HD), D ** -0.5, 0.046875, ((0, 8), (1, 8))),
        "w_keyval": normal_values(streams_of[2], (D, 2 * KVH * HD), D ** -0.5, 0.046875, ((0, 8), (1, 8))),
        "w_out": normal_values(streams_of[3], (HQ * HD, D), (HQ * HD) ** -0.5, 0.0625, ((0, 8), (1, 8))),
        "kv_pages": draw_kv_pages(jax.random.fold_in(streams_of[7], 71), 0),
        "page_slot": draw_page_slot(jax.random.fold_in(streams_of[7], 71), 0),
        "lengths": ragged_sizes(streams_of[6], ROWS, ROWS * RES // 2, RES, 0).astype(jnp.int32),
    }


def rounded(values):
    return lax.optimization_barrier(values.astype(jnp.bfloat16)).astype(jnp.float32)


def blockwise(inputs, weights, blocks):
    block_width = inputs.shape[1] // blocks
    running = jnp.zeros((inputs.shape[0], weights.shape[1]), jnp.float32)
    for number in range(blocks):
        product = jnp.dot(inputs[:, number * block_width:(number + 1) * block_width],
                          weights[number * block_width:(number + 1) * block_width],
                          preferred_element_type=jnp.float32)
        running = running + product
    return running


def prefill_head(query_head, context_keys, context_values, recent_keys, recent_values):
    score_scale = HD ** -0.5
    context_scores = jnp.einsum("rgd,sd->rgs", query_head.astype(jnp.float32), context_keys.astype(jnp.float32)) * score_scale
    recent_scores = jnp.einsum("rgd,jd->rgj", query_head.astype(jnp.float32), recent_keys.astype(jnp.float32)) * score_scale
    allowed = jnp.arange(ROWS)[None, None, :] <= jnp.arange(ROWS)[:, None, None]
    recent_scores = jnp.where(allowed, recent_scores, -jnp.inf)
    largest = jnp.maximum(jnp.max(context_scores, axis=2), jnp.max(recent_scores, axis=2))
    context_weights = jnp.exp(context_scores - largest[:, :, None])
    recent_weights = jnp.exp(recent_scores - largest[:, :, None])
    totals = jnp.sum(context_weights, axis=2) + jnp.sum(recent_weights, axis=2)
    mixture = jnp.einsum("rgs,sd->rgd", rounded(context_weights), context_values.astype(jnp.float32))
    mixture = mixture + jnp.einsum("rgj,jd->rgd", rounded(recent_weights), recent_values.astype(jnp.float32))
    return (mixture / totals[:, :, None]).astype(jnp.bfloat16)


def prefill(query_rows, keyval_rows, context_pages):
    queries = query_rows.reshape(ROWS, KVH, GROUP_Q, HD).transpose(1, 0, 2, 3)
    context = context_pages.reshape(DEPTH, KVH, 2, HD).transpose(1, 2, 0, 3)
    recent_pair = keyval_rows.reshape(ROWS, KVH, 2, HD).transpose(1, 2, 0, 3)

    def one_head(pieces):
        return prefill_head(pieces[0], pieces[1][0], pieces[1][1], pieces[2][0], pieces[2][1])

    head_out = lax.map(one_head, (queries, context, recent_pair))
    return head_out.transpose(1, 0, 2, 3).reshape(ROWS, HQ * HD)


def decode_rows(query_rows, keyval_rows, resident, relaid_pool, lengths):
    score_scale = HD ** -0.5
    queries = query_rows.reshape(ROWS, KVH, GROUP_Q, HD).astype(jnp.float32)
    own_pair = keyval_rows.reshape(ROWS, KVH, 2, HD).astype(jnp.float32)
    resident_pair = resident.reshape(ROWS, RES, KVH, 2, HD).astype(jnp.float32)
    relaid_pair = relaid_pool.reshape(ROWS, RES, KVH, 2, HD).astype(jnp.float32)
    live_mask = jnp.arange(RES)[None, :] < lengths[:, None]
    resident_scores = jnp.einsum("rkgd,rskd->rkgs", queries, resident_pair[:, :, :, 0]) * score_scale
    resident_scores = jnp.where(live_mask[:, None, None, :], resident_scores, -jnp.inf)
    relaid_scores = jnp.einsum("rkgd,rskd->rkgs", queries, relaid_pair[:, :, :, 0]) * score_scale
    own_scores = jnp.einsum("rkgd,rkd->rkg", queries, own_pair[:, :, 0]) * score_scale
    largest = jnp.maximum(jnp.maximum(jnp.max(resident_scores, axis=3), jnp.max(relaid_scores, axis=3)), own_scores)
    resident_weights = jnp.exp(resident_scores - largest[..., None])
    relaid_weights = jnp.exp(relaid_scores - largest[..., None])
    own_weights = jnp.exp(own_scores - largest)
    totals = jnp.sum(resident_weights, axis=3) + jnp.sum(relaid_weights, axis=3) + own_weights
    mixture = jnp.einsum("rkgs,rskd->rkgd", rounded(resident_weights), resident_pair[:, :, :, 1])
    mixture = mixture + jnp.einsum("rkgs,rskd->rkgd", rounded(relaid_weights), relaid_pair[:, :, :, 1])
    mixture = mixture + rounded(own_weights)[..., None] * own_pair[:, :, None, 1]
    return (mixture / totals[..., None]).astype(jnp.bfloat16).reshape(ROWS, HQ * HD)


def reference(hidden_in, w_query, w_keyval, w_out, kv_pages, page_slot, lengths):
    flat_rows = hidden_in.reshape(2 * ROWS, D)
    query_rows = blockwise(flat_rows, w_query, N_CTX).astype(jnp.bfloat16).reshape(2, ROWS, HQ * HD)
    keyval = blockwise(flat_rows, w_keyval, N_CTX).astype(jnp.bfloat16).reshape(2, ROWS, 2 * KVH * HD)
    relaid_pool = jnp.zeros_like(kv_pages[0]).at[page_slot].set(kv_pages[0])
    page_pools = jnp.stack([kv_pages[0], relaid_pool])
    prefill_heads = prefill(query_rows[0], keyval[0], kv_pages[0])
    decode_heads = decode_rows(query_rows[1], keyval[1], kv_pages[1], relaid_pool, lengths)
    all_heads = jnp.stack([prefill_heads, decode_heads]).reshape(2 * ROWS, HQ * HD)
    attn_out = blockwise(all_heads, w_out, N_TP).astype(jnp.bfloat16)
    return (attn_out.reshape(2, ROWS, D), page_pools)
```

```python
import functools
import math

import jax
import jax.numpy as jnp
from jax import lax
from jax.experimental import pallas as pl
from jax.experimental.pallas import tpu as pltpu
from jax.sharding import PartitionSpec as P

HD = 128
HEADS = 8
CTX = 8
ROW = 64
STEPS = ((0, 0), (0, 1), (0, 3), (1, 0), (1, 1), (1, 3), (0, 2), (1, 2))
COEF = HD ** -0.5 * math.log2(math.e)
BF = jnp.bfloat16
F32 = jnp.float32
QKV_SEND = F32
SMEM = pl.BlockSpec(memory_space=pltpu.SMEM)
VMEM = pl.BlockSpec(memory_space=pltpu.VMEM)
ANY = pl.BlockSpec(memory_space=pl.ANY)
PREFILL, ME, TO, FROM, SENDS, PLACE = 0, 1, 8, 16, 24, 32


def peer(place, step, sign):
    flip, turn = step
    return (place // 4 ^ flip) * 4 + (place + sign * turn) % 4


def table():
    ctx = lax.axis_index("ctx")
    tp = lax.axis_index("tp")
    flips = jnp.array([s[0] for s in STEPS], jnp.int32)
    turns = jnp.array([s[1] for s in STEPS], jnp.int32)
    to = (ctx // 4 ^ flips) * 4 + (ctx + turns) % 4
    origin = (ctx // 4 ^ flips) * 4 + (ctx + 4 - turns) % 4
    head = jnp.stack(
        [(lax.axis_index("group") == 0).astype(jnp.int32), ctx, tp] + [jnp.int32(0)] * 5
    )
    sends = (origin % 2 != tp % 2).astype(jnp.int32)
    place = (origin // 2 + 4 - tp // 2) % 4
    return jnp.concatenate([head, to, origin, sends, place]).astype(jnp.int32)


def params(limit=48 << 20, **more):
    return pltpu.CompilerParams(vmem_limit_bytes=limit, **more)


def nbytes(*arrays):
    return sum(math.prod(a.shape) * a.dtype.itemsize for a in arrays)


def project_kernel(meta, x, wq, wkv, *rest):
    outs, acc = rest[:CTX], rest[CTX]
    k = pl.program_id(0)
    wide = wq.shape[1]
    part_q = jnp.dot(x[...], wq[...], preferred_element_type=F32)
    part_kv = jnp.dot(x[...], wkv[...], preferred_element_type=F32)

    @pl.when(k == 0)
    def _():
        acc[:, :wide] = part_q
        acc[:, wide:] = part_kv

    @pl.when(k > 0)
    def _():
        acc[:, :wide] += part_q
        acc[:, wide:] += part_kv

    @pl.when(k == pl.num_programs(0) - 1)
    def _():
        for s in range(CTX):
            first = pl.multiple_of(meta[TO + s] * ROW, ROW)
            outs[s][...] = acc[pl.ds(first, ROW), :].astype(outs[s].dtype)


def project(meta, tokens, w_query, w_keyval):
    rows, depth = tokens.shape
    wide = w_query.shape[1]
    both = wide + w_keyval.shape[1]
    blocks = 4
    deep = depth // blocks
    return pl.pallas_call(
        project_kernel,
        grid=(blocks,),
        in_specs=[
            SMEM,
            pl.BlockSpec((rows, deep), lambda k: (0, k)),
            pl.BlockSpec((deep, wide), lambda k: (k, 0)),
            pl.BlockSpec((deep, both - wide), lambda k: (k, 0)),
        ],
        out_specs=[pl.BlockSpec((ROW, both), lambda k: (0, 0))] * CTX,
        out_shape=[jax.ShapeDtypeStruct((ROW, both), F32 if s == 0 else QKV_SEND) for s in range(CTX)],
        scratch_shapes=[pltpu.VMEM((rows, both), F32)],
        compiler_params=params(),
        cost_estimate=pl.CostEstimate(
            flops=2 * rows * depth * both, bytes_accessed=nbytes(tokens, w_query, w_keyval), transcendentals=0
        ),
        name="project",
    )(meta, tokens, w_query, w_keyval)


def add_kernel(*refs):
    parts, q, kv = refs[:CTX], refs[CTX], refs[CTX + 1]
    total = parts[0][...]
    for part in parts[1:]:
        total = total + part[...].astype(F32)
    total = total.astype(BF)
    q[...] = total[:, : HEADS * HD]
    kv[...] = total[:, HEADS * HD :]


def add_parts(parts):
    return pl.pallas_call(
        add_kernel,
        in_specs=[VMEM] * CTX,
        out_specs=[VMEM] * 2,
        out_shape=[
            jax.ShapeDtypeStruct((ROW, HEADS * HD), BF),
            jax.ShapeDtypeStruct((ROW, 2 * HD), BF),
        ],
        compiler_params=params(),
        cost_estimate=pl.CostEstimate(flops=8 * 64 * 1280, bytes_accessed=nbytes(*parts), transcendentals=0),
        name="add_parts",
    )(*parts)


def sort_kernel(meta, slots, pages, *rest):
    outs, arrivals, counts, order, sem = rest[:CTX], rest[CTX], rest[CTX + 1], rest[CTX + 2], rest[CTX + 3]
    me = meta[ME]
    per = 8

    def clear(i, _):
        counts[i] = 0
        return 0

    @pl.when(meta[PREFILL] == 1)
    def _():
        lax.fori_loop(0, CTX, clear, 0)

        def place(i, _):
            target = lax.shift_right_logical(slots[me * 64 + i], 6)
            n = counts[target]
            order[target * per + n] = i
            counts[target] = n + 1
            return 0

        lax.fori_loop(0, 64, place, 0)
        for s in range(CTX):
            to = meta[TO + s]
            for n in range(per):
                pltpu.make_async_copy(pages.at[order[to * per + n]], outs[s].at[n], sem).start()
        for s in range(CTX):
            pltpu.make_async_copy(pages.at[pl.ds(0, per)], outs[s], sem).wait()

    @pl.when(meta[PREFILL] == 0)
    def _():
        lax.fori_loop(0, CTX, clear, 0)
        for s in range(CTX):
            origin = meta[FROM + s]

            def place(i, n):
                slot = slots[origin * 64 + i]
                mine = lax.shift_right_logical(slot, 6) == me

                @pl.when(mine)
                def _():
                    arrivals[s * per + n] = lax.bitwise_and(slot, 63)

                return n + mine.astype(jnp.int32)

            lax.fori_loop(0, 64, place, 0)


def sort_pages(meta, page_slot, pages):
    chunk = jax.ShapeDtypeStruct((8,) + pages.shape[1:], pages.dtype)
    return pl.pallas_call(
        sort_kernel,
        in_specs=[SMEM, SMEM, ANY],
        out_specs=[ANY] * CTX + [SMEM],
        out_shape=[chunk] * CTX + [jax.ShapeDtypeStruct((64,), jnp.int32)],
        scratch_shapes=[pltpu.SMEM((CTX,), jnp.int32), pltpu.SMEM((64,), jnp.int32), pltpu.SemaphoreType.DMA],
        compiler_params=params(4 << 20),
        cost_estimate=pl.CostEstimate(flops=0, bytes_accessed=2 * nbytes(pages), transcendentals=0),
        name="sort_pages",
    )(meta, page_slot, pages)


def weigh(scores, values, m, l, acc):
    new = jnp.maximum(m[...], jnp.max(scores, axis=1, keepdims=True))
    fade = jnp.exp2((m[...] - new) * COEF)
    weights = jnp.exp2((scores - new[:, :1]) * COEF)
    l[...] = l[...] * fade + jnp.sum(weights, axis=1, keepdims=True)
    acc[...] = acc[...] * fade + jnp.dot(weights.astype(BF), values, preferred_element_type=F32)
    m[...] = new


def attend_kernel(step, meta, q, kv, own, out, q2, m, l, acc):
    j = pl.program_id(0)
    contract = (((1,), (1,)), ((), ()))

    @pl.when(meta[PREFILL] == 1)
    def _():
        @pl.when(j == 0)
        def _():
            for h in range(HEADS):
                q2[pl.ds(h * ROW, ROW), :] = q[:, h * HD : (h + 1) * HD]
            m[...] = jnp.full_like(m, -1e30)
            l[...] = jnp.zeros_like(l)
            acc[...] = jnp.zeros_like(acc)

        scores = lax.dot_general(q2[...], kv[:, :HD], contract, preferred_element_type=F32)
        weigh(scores, kv[:, HD:], m, l, acc)

        @pl.when(j == pl.num_programs(0) - 1)
        def _():
            ahead = (meta[FROM + step] - meta[ME]) * ROW
            scores = lax.dot_general(q2[...], own[:, :HD], contract, preferred_element_type=F32)
            token = lax.bitwise_and(lax.broadcasted_iota(jnp.int32, scores.shape, 0), ROW - 1)
            key = lax.broadcasted_iota(jnp.int32, scores.shape, 1)
            scores = jnp.where(key <= token + ahead, scores, -1e30)
            weigh(scores, own[:, HD:], m, l, acc)
            mixed = acc[...] / l[...]
            level = m[...] * COEF + jnp.log2(l[...])
            high = level.astype(BF).astype(F32)
            rest = level - high
            mid = rest.astype(BF).astype(F32)
            low = rest - mid
            lane = lax.broadcasted_iota(jnp.int32, (ROW, HD), 1)
            stats = jnp.zeros((ROW, HD), F32)
            for h in range(HEADS):
                rows = slice(h * ROW, (h + 1) * ROW)
                out[:, h * HD : (h + 1) * HD] = mixed[rows].astype(out.dtype)
                stats = jnp.where(lane == 3 * h, high[rows], stats)
                stats = jnp.where(lane == 3 * h + 1, mid[rows], stats)
                stats = jnp.where(lane == 3 * h + 2, low[rows], stats)
            out[:, HEADS * HD :] = stats.astype(out.dtype)


def attend(step, meta, q, pages, own, block=1024):
    keys = pages.shape[0]
    big = HEADS * ROW
    return pl.pallas_call(
        functools.partial(attend_kernel, step),
        grid=(keys // block,),
        in_specs=[
            SMEM,
            pl.BlockSpec((ROW, HEADS * HD), lambda j: (0, 0)),
            pl.BlockSpec((block, 2 * HD), lambda j: (j, 0)),
            pl.BlockSpec((ROW, 2 * HD), lambda j: (0, 0)),
        ],
        out_specs=pl.BlockSpec((ROW, (HEADS + 1) * HD), lambda j: (0, 0)),
        out_shape=jax.ShapeDtypeStruct((ROW, (HEADS + 1) * HD), F32 if step == 0 else BF),
        scratch_shapes=[
            pltpu.VMEM((big, HD), BF),
            pltpu.VMEM((big, HD), F32),
            pltpu.VMEM((big, HD), F32),
            pltpu.VMEM((big, HD), F32),
        ],
        compiler_params=params(),
        cost_estimate=pl.CostEstimate(
            flops=4 * big * keys * HD, bytes_accessed=nbytes(pages), transcendentals=big * keys
        ),
        name=f"attend_{step}",
    )(meta, q, pages, own)


def finish_kernel(meta, lengths, arrivals, q, own, *rest):
    states, pages, chunks = rest[:CTX], rest[CTX], rest[CTX + 1 : 2 * CTX + 1]
    heads, pool = rest[2 * CTX + 1 : 2 * CTX + 3]
    held, relaid, q3, o3, sems = rest[2 * CTX + 3 :]
    contract = (((1,), (1,)), ((), ()))
    per = 8

    @pl.when(meta[PREFILL] == 1)
    def _():
        copy = pltpu.make_async_copy(pages, pool, sems.at[0])
        copy.start()
        for h in range(HEADS):
            cols = slice(h * HD, (h + 1) * HD)
            levels = []
            for state in states:
                three = state[:, HEADS * HD :].astype(F32)[:, 3 * h : 3 * h + 3]
                levels.append(three[:, 0:1] + three[:, 1:2] + three[:, 2:3])
            top = functools.reduce(jnp.maximum, levels)
            parts = [jnp.exp2(level - top) for level in levels]
            mixed = sum(state[:, cols].astype(F32) * part for state, part in zip(states, parts))
            heads[:, cols] = (mixed / sum(parts)).astype(BF)
        copy.wait()

    @pl.when(meta[PREFILL] == 0)
    def _():
        load = pltpu.make_async_copy(pages, held, sems.at[0])
        load.start()
        for s in range(CTX):
            for n in range(per):
                slot = arrivals[s * per + n]
                pltpu.make_async_copy(chunks[s].at[n], relaid.at[slot], sems.at[1]).start()
                pltpu.make_async_copy(chunks[s].at[n], pool.at[slot], sems.at[2]).start()
        for h in range(HEADS):
            q3[:, h, :] = q[:, h * HD : (h + 1) * HD].astype(F32)
        load.wait()
        pltpu.make_async_copy(pages, relaid, sems.at[1]).wait()
        at_once = 8
        lane = lax.broadcasted_iota(jnp.int32, (HEADS, 2 * ROW), 1)

        def some(i, _):
            first = i * at_once
            own_rows = own[pl.ds(pl.multiple_of(first, at_once), at_once), :].astype(F32)
            scores, own_scores, values = [], [], []
            for r in range(at_once):
                both = jnp.concatenate([held[first + r], relaid[first + r]], axis=0)
                queries = q3[first + r]
                s = lax.dot_general(queries.astype(BF), both[:, :HD], contract, preferred_element_type=F32)
                seen = (lane < lengths[first + r]) | (lane >= ROW)
                scores.append(jnp.where(seen, s, -1e30))
                own_scores.append(jnp.sum(queries * own_rows[r : r + 1, :HD], axis=1, keepdims=True))
                values.append(both[:, HD:])
            scores = jnp.concatenate(scores, axis=0)
            own_scores = jnp.concatenate(own_scores, axis=0)
            top = jnp.maximum(jnp.max(scores, axis=1, keepdims=True), own_scores)
            weights = jnp.exp2((scores - top) * COEF)
            own_weights = jnp.exp2((own_scores - top) * COEF)
            total = jnp.sum(weights, axis=1, keepdims=True) + own_weights
            weights = weights.astype(BF)
            own_weights = own_weights.astype(BF).astype(F32)
            for r in range(at_once):
                rows = slice(r * HEADS, (r + 1) * HEADS)
                mixed = jnp.dot(weights[rows], values[r], preferred_element_type=F32)
                mixed = mixed + own_weights[rows] * own_rows[r : r + 1, HD:]
                o3[first + r] = mixed / total[rows]
            return 0

        lax.fori_loop(0, ROW // at_once, some, 0)
        for h in range(HEADS):
            heads[:, h * HD : (h + 1) * HD] = o3[:, h, :].astype(BF)
        pltpu.make_async_copy(pages, pool, sems.at[2]).wait()


def finish(meta, lengths, arrivals, q, own, states, pages, chunks):
    return pl.pallas_call(
        finish_kernel,
        in_specs=[SMEM] * 3 + [VMEM] * (2 + CTX) + [ANY] * (1 + CTX),
        out_specs=[VMEM, ANY],
        out_shape=[
            jax.ShapeDtypeStruct((ROW, HEADS * HD), BF),
            jax.ShapeDtypeStruct(pages.shape, BF),
        ],
        scratch_shapes=[
            pltpu.VMEM(pages.shape, BF),
            pltpu.VMEM(pages.shape, BF),
            pltpu.VMEM((ROW, HEADS, HD), F32),
            pltpu.VMEM((ROW, HEADS, HD), F32),
            pltpu.SemaphoreType.DMA((3,)),
        ],
        compiler_params=params(),
        cost_estimate=pl.CostEstimate(flops=1 << 24, bytes_accessed=3 * nbytes(pages), transcendentals=1 << 16),
        name="finish",
    )(meta, lengths, arrivals, q, own, *states, pages, *chunks)


def gather_rows(meta, chunks, rows, wanted):
    for s in range(CTX):
        @pl.when(meta[SENDS + s] == wanted)
        def _():
            rows[pl.ds(pl.multiple_of(meta[PLACE + s] * ROW, ROW), ROW), :] = chunks[s][...]


def other_half_kernel(meta, *rest):
    chunks, w, out, rows = rest[:CTX], rest[CTX], rest[CTX + 1], rest[CTX + 2]

    @pl.when(pl.program_id(0) == 0)
    def _():
        gather_rows(meta, chunks, rows, 1)

    out[...] = jnp.dot(rows[...], w[...], preferred_element_type=F32).astype(BF)


def own_half_kernel(meta, *rest):
    chunks, w, came, rows = rest[:CTX], rest[CTX], rest[CTX + 1], rest[-1]
    outs = rest[CTX + 2 : CTX + 6]

    @pl.when(pl.program_id(0) == 0)
    def _():
        gather_rows(meta, chunks, rows, 0)

    total = jnp.dot(rows[...], w[...], preferred_element_type=F32) + came[...].astype(F32)
    for p in range(4):
        outs[p][...] = total[p * ROW : (p + 1) * ROW].astype(outs[p].dtype)


def out_specs_of(chunks, w_out, block):
    wide = w_out.shape[0]
    return [SMEM] + [pl.BlockSpec((ROW, wide), lambda n: (0, 0))] * CTX + [
        pl.BlockSpec((wide, block), lambda n: (0, n))
    ]


def other_half(meta, chunks, w_out, block=512):
    depth, wide = w_out.shape
    return pl.pallas_call(
        other_half_kernel,
        grid=(wide // block,),
        in_specs=out_specs_of(chunks, w_out, block),
        out_specs=pl.BlockSpec((4 * ROW, block), lambda n: (0, n)),
        out_shape=jax.ShapeDtypeStruct((4 * ROW, wide), BF),
        scratch_shapes=[pltpu.VMEM((4 * ROW, depth), BF)],
        compiler_params=params(),
        cost_estimate=pl.CostEstimate(
            flops=8 * ROW * depth * wide, bytes_accessed=nbytes(w_out), transcendentals=0
        ),
        name="other_half",
    )(meta, *chunks, w_out)


def own_half(meta, chunks, w_out, came, block=512):
    depth, wide = w_out.shape
    return pl.pallas_call(
        own_half_kernel,
        grid=(wide // block,),
        in_specs=out_specs_of(chunks, w_out, block) + [pl.BlockSpec((4 * ROW, block), lambda n: (0, n))],
        out_specs=[pl.BlockSpec((ROW, block), lambda n: (0, n))] * 4,
        out_shape=[jax.ShapeDtypeStruct((ROW, wide), F32 if p == 0 else BF) for p in range(4)],
        scratch_shapes=[pltpu.VMEM((4 * ROW, depth), BF)],
        compiler_params=params(),
        cost_estimate=pl.CostEstimate(
            flops=8 * ROW * depth * wide, bytes_accessed=nbytes(w_out), transcendentals=0
        ),
        name="own_half",
    )(meta, *chunks, w_out, came)


def last_kernel(a, b, c, d, out):
    out[...] = (a[...] + b[...].astype(F32) + c[...].astype(F32) + d[...].astype(F32)).astype(BF)


def last_sum(parts):
    return pl.pallas_call(
        last_kernel,
        in_specs=[VMEM] * 4,
        out_specs=VMEM,
        out_shape=jax.ShapeDtypeStruct(parts[0].shape, BF),
        compiler_params=params(),
        cost_estimate=pl.CostEstimate(flops=1 << 19, bytes_accessed=nbytes(*parts), transcendentals=0),
        name="last_sum",
    )(*parts)


def shards(hidden_in, w_query, w_keyval, w_out, kv_pages, page_slot, lengths):
    meta = table()
    pages = kv_pages[0]
    flat_pages = pages.reshape(-1, pages.shape[2])

    def ring(value, s, sign=1):
        return lax.ppermute(value, "ctx", [(c, peer(c, STEPS[s], sign)) for c in range(CTX)])

    parts = project(meta, hidden_in[0], w_query, w_keyval)
    parts = [parts[0]] + [ring(parts[s], s) for s in range(1, CTX)]
    *sorted_pages, arrivals = sort_pages(meta, page_slot, pages)
    chunks = [
        lax.ppermute(
            sorted_pages[s], ("group", "ctx"), [(c, CTX + peer(c, STEPS[s], 1)) for c in range(CTX)]
        )
        for s in range(CTX)
    ]
    q, own = add_parts(parts)
    states = [attend(0, meta, q, flat_pages, own)]
    for s in range(1, CTX):
        came = ring(q, s)
        states.append(ring(attend(s, meta, came, flat_pages, own), s, -1))
    heads, pool = finish(meta, lengths, arrivals, q, own, states, pages, chunks)
    gathered = [heads] + [ring(heads, s) for s in range(1, CTX)]
    sent = other_half(meta, gathered, w_out)
    came = lax.ppermute(sent, "tp", [(t, t ^ 1) for t in range(8)])
    mine = own_half(meta, gathered, w_out, came)
    totals = [mine[0]] + [
        lax.ppermute(mine[p], "tp", [(t, (t + 2 * p) % 8) for t in range(8)]) for p in range(1, 4)
    ]
    return (last_sum(totals)[None], pool[None])


def solution(mesh):
    placed = (
        P("group", None, "ctx"),
        P("ctx", "tp"),
        P("ctx", "tp"),
        P("tp", "ctx"),
        P("group", "ctx", None, "tp"),
        P(),
        P("ctx"),
    )
    return jax.shard_map(
        shards,
        mesh=mesh,
        in_specs=placed,
        out_specs=(P("group", "tp", "ctx"), P("group", "ctx", None, "tp")),
        check_vma=False,
    )
```

```python
import functools
import math

import jax
import jax.numpy as jnp
from jax import lax
from jax.experimental import pallas as pl
from jax.experimental.pallas import tpu as pltpu
from jax.sharding import PartitionSpec as P

HD = 128
HEADS = 8
STATE = (HEADS + 1) * HD
CTX = 8
ROW = 64
STEPS = ((0, 0), (1, 0), (0, 1), (0, 3), (1, 1), (1, 3), (0, 2), (1, 2))
COEF = HD ** -0.5 * math.log2(math.e)
BF = jnp.bfloat16
F32 = jnp.float32
F16 = jnp.float16
LIFT = 64.0
SMEM = pl.BlockSpec(memory_space=pltpu.SMEM)
VMEM = pl.BlockSpec(memory_space=pltpu.VMEM)
ANY = pl.BlockSpec(memory_space=pl.ANY)
PREFILL, ME, TP = 0, 1, 2


def peer(place, step, sign):
    flip, turn = step
    return (place // 4 ^ flip) * 4 + (place + sign * turn) % 4


def place_here():
    return jnp.stack([1 - lax.axis_index("group"), lax.axis_index("ctx"), lax.axis_index("tp")]).astype(jnp.int32)


def params(limit=24 << 20, **more):
    return pltpu.CompilerParams(vmem_limit_bytes=limit, **more)


def nbytes(*arrays):
    return sum(math.prod(a.shape) * a.dtype.itemsize for a in arrays)


def pages_for(slots, holder, target, found):
    origin = lax.bitwise_xor(holder, 4)

    def look(i, n):
        slot = slots[origin * 64 + i]
        there = lax.shift_right_logical(slot, 6) == target

        @pl.when(there)
        def _():
            found(n, i, lax.bitwise_and(slot, 63))

        return n + there.astype(jnp.int32)

    lax.fori_loop(0, 64, look, jnp.int32(0), unroll=4)


def places(meta, slots, spots):
    me = meta[ME]
    for step in range(CTX):
        def coming(n, page, slot):
            spots[step * 8 + n] = slot

        def leaving(n, page, slot):
            spots[64 + step * 8 + n] = page

        pages_for(slots, peer(me, STEPS[step], 1), me, coming)
        pages_for(slots, me, peer(me, STEPS[step], -1), leaving)


def weigh(scores, values, state):
    m, l, acc = state
    new = jnp.maximum(m, jnp.max(scores, axis=1, keepdims=True))
    fade = jnp.exp2((m - new) * COEF)
    weights = jnp.exp2((scores - new) * COEF)
    lanes = [weights[:, x : x + HD] for x in range(0, weights.shape[1], HD)]
    l = l * fade + functools.reduce(jnp.add, lanes)
    acc = acc * fade + jnp.dot(weights.astype(BF), values, preferred_element_type=F32)
    return (new, l, acc)


def attend_rows(meta, owner, block, q, kv, mine, out, q2, pair):
    contract = (((1,), (1,)), ((), ()))
    big = HEADS * ROW
    if q is not None:
        for h in range(HEADS):
            q2[h * ROW : (h + 1) * ROW, :] = q[:, h * HD : (h + 1) * HD]
    pair[:ROW, :] = mine[:, HEADS * HD :]
    pair[ROW:, :] = jnp.zeros((HD - ROW, 2 * HD), BF)
    ahead = (owner - meta[ME]) * ROW
    scores = lax.dot_general(q2[...], pair[:, :HD], contract, preferred_element_type=F32)
    token = lax.bitwise_and(lax.broadcasted_iota(jnp.int32, scores.shape, 0), ROW - 1)
    key = lax.broadcasted_iota(jnp.int32, scores.shape, 1)
    scores = jnp.where((key <= token + ahead) & (key < ROW), scores, -1e30)
    state = (
        jnp.full((big, 1), -1e30, F32),
        jnp.zeros((big, HD), F32),
        jnp.zeros((big, HD), F32),
    )
    state = weigh(scores, pair[:, HD:], state)
    for first in range(0, kv.shape[0], block):
        some = slice(first, first + block)
        scores = lax.dot_general(q2[...], kv[some, :HD], contract, preferred_element_type=F32)
        state = weigh(scores, kv[some, HD:], state)
    m, l, acc = state
    l = jnp.sum(l, axis=1, keepdims=True)
    mixed = acc * (1.0 / l)
    level = m * COEF + jnp.log2(l)
    high = level.astype(BF).astype(F32)
    rest = level - high
    mid = rest.astype(BF).astype(F32)
    low = rest - mid
    lane = lax.broadcasted_iota(jnp.int32, (ROW, HD), 1)
    stats = jnp.zeros((ROW, HD), F32)
    for h in range(HEADS):
        rows = slice(h * ROW, (h + 1) * ROW)
        out[:, h * HD : (h + 1) * HD] = mixed[rows].astype(out.dtype)
        stats = jnp.where(lane == h, high[rows], stats)
        stats = jnp.where(lane == 8 + h, mid[rows], stats)
        stats = jnp.where(lane == 16 + h, low[rows], stats)
    out[:, HEADS * HD :] = stats.astype(out.dtype)


def plan_kernel(meta, slots, spots):
    @pl.when(meta[PREFILL] == 0)
    def _():
        places(meta, slots, spots)


def plan(meta, slots):
    return pl.pallas_call(
        plan_kernel,
        in_specs=[SMEM] * 2,
        out_specs=SMEM,
        out_shape=jax.ShapeDtypeStruct((128,), jnp.int32),
        compiler_params=params(),
        cost_estimate=pl.CostEstimate(flops=0, bytes_accessed=0, transcendentals=0),
        name="plan",
    )(meta, slots)


def own_kernel(block, meta, mine, kv, after, out, q2, pair):
    @pl.when(meta[PREFILL] == 1)
    def _():
        attend_rows(meta, meta[ME], block, mine, kv, mine, out, q2, pair)


def attend_own(meta, mine, pages, after, block=2048):
    big = HEADS * ROW
    return pl.pallas_call(
        functools.partial(own_kernel, block),
        in_specs=[SMEM] + [VMEM] * 2 + [ANY],
        out_specs=VMEM,
        out_shape=jax.ShapeDtypeStruct((ROW, STATE), F32),
        scratch_shapes=[pltpu.VMEM((big, HD), BF), pltpu.VMEM((HD, 2 * HD), BF)],
        compiler_params=params(),
        cost_estimate=pl.CostEstimate(flops=1 << 32, bytes_accessed=0, transcendentals=0),
        name="attend_own",
    )(meta, mine, pages, after)


def attend_kernel(steps, block, meta, spots, crossed, kv, mine, *rest):
    queries, outs, (state, q2, pair, sem) = rest[: len(steps)], rest[-len(steps) - 4 : -4], rest[-4:]
    i = pl.program_id(0)

    @pl.when(meta[PREFILL] == 1)
    def _():
        attend_step(meta, steps, block, queries, kv, mine, outs, state, q2, pair)

    @pl.when((meta[PREFILL] == 0) & (i == 0))
    def _():
        fill_pages(steps, spots, crossed, outs, sem)


def attend_step(meta, steps, block, queries, kv, mine, outs, state, q2, pair):
    i = pl.program_id(0)
    owner = jnp.int32(0)
    for n, step in enumerate(steps):
        owner = jnp.where(i == n, peer(meta[ME], STEPS[step], -1), owner)
        @pl.when(i == n)
        def _():
            for h in range(HEADS):
                q2[h * ROW : (h + 1) * ROW, :] = queries[n][:, h * HD : (h + 1) * HD]
    attend_rows(meta, owner, block, None, kv, mine, state, q2, pair)
    for n in range(len(steps)):
        @pl.when(i == n)
        def _():
            outs[n][:, :STATE] = state[...]


def attend_scratch():
    return [
        pltpu.VMEM((ROW, STATE), BF),
        pltpu.VMEM((HEADS * ROW, HD), BF),
        pltpu.VMEM((HD, 2 * HD), BF),
    ]


def attend(steps, meta, spots, crossed, pages, mine, queries, after, block=2048):
    return pl.pallas_call(
        functools.partial(attend_kernel, steps, block),
        grid=(len(steps),),
        in_specs=[SMEM] * 2 + [ANY] + [VMEM] * (2 + len(queries)) + [ANY] * len(after),
        out_specs=[VMEM] * len(steps),
        out_shape=[jax.ShapeDtypeStruct((ROW, 16 * HD), BF)] * len(steps),
        scratch_shapes=attend_scratch() + [pltpu.SemaphoreType.DMA((len(steps), 8))],
        compiler_params=params(),
        cost_estimate=pl.CostEstimate(flops=len(steps) << 32, bytes_accessed=0, transcendentals=0),
        name=f"attend_{steps[0]}",
    )(meta, spots, crossed, pages, mine, *queries, *after)


def start_kernel(steps, block, meta, kv, mine, *rest):
    queries, outs, (pool, state, q2, pair, sem) = rest[: len(steps)], rest[-len(steps) - 5 : -5], rest[-5:]
    i = pl.program_id(0)

    @pl.when(meta[PREFILL] == 1)
    def _():
        keep = pltpu.make_async_copy(kv, pool, sem)

        @pl.when(i == 0)
        def _():
            keep.start()

        attend_step(meta, steps, block, queries, kv, mine, outs, state, q2, pair)

        @pl.when(i == len(steps) - 1)
        def _():
            keep.wait()


def attend_first(steps, meta, pages, mine, queries, block=2048):
    return pl.pallas_call(
        functools.partial(start_kernel, steps, block),
        grid=(len(steps),),
        in_specs=[SMEM] + [VMEM] * (2 + len(queries)),
        out_specs=[VMEM] * len(steps) + [ANY],
        out_shape=[jax.ShapeDtypeStruct((ROW, 16 * HD), BF)] * len(steps)
        + [jax.ShapeDtypeStruct(pages.shape, BF)],
        scratch_shapes=attend_scratch() + [pltpu.SemaphoreType.DMA],
        compiler_params=params(),
        cost_estimate=pl.CostEstimate(flops=0, bytes_accessed=0, transcendentals=0),
        name=f"attend_{steps[0]}",
    )(meta, pages, mine, *queries)


def fill_pages(steps, spots, crossed, outs, sem):
    copies = [
        pltpu.make_async_copy(
            crossed.at[spots[64 + step * 8 + p]], outs[n].at[:, p * 2 * HD : (p + 1) * 2 * HD], sem.at[n, p]
        )
        for n, step in enumerate(steps)
        for p in range(8)
    ]
    for copy in copies:
        copy.start()
    for copy in copies:
        copy.wait()


def fill_kernel(steps, meta, spots, crossed, *rest):
    outs, sem = rest[len(steps) : -1], rest[-1]

    @pl.when(meta[PREFILL] == 0)
    def _():
        fill_pages(steps, spots, crossed, outs, sem)


def fill(steps, meta, spots, crossed, values):
    return pl.pallas_call(
        functools.partial(fill_kernel, steps),
        in_specs=[SMEM] * 2 + [ANY] + [VMEM] * len(steps),
        out_specs=[VMEM] * len(steps),
        out_shape=[jax.ShapeDtypeStruct(value.shape, BF) for value in values],
        scratch_shapes=[pltpu.SemaphoreType.DMA((len(steps), 8))],
        input_output_aliases={3 + n: n for n in range(len(steps))},
        compiler_params=params(),
        cost_estimate=pl.CostEstimate(flops=0, bytes_accessed=0, transcendentals=0),
        name=f"fill_{steps[0]}",
    )(meta, spots, crossed, *values)


def finish_kernel(meta, spots, lengths, mine, *rest):
    came, (pages, crossed, _, heads, pool, held, relaid, q3, o3, sems) = rest[:CTX], rest[CTX:]
    contract = (((1,), (1,)), ((), ()))

    @pl.when(meta[PREFILL] == 1)
    def _():
        levels = []
        for j in range(CTX):
            stats = came[j][:, HEADS * HD : STATE].astype(F32)
            levels.append(stats + pltpu.roll(stats, HD - 8, 1) + pltpu.roll(stats, HD - 16, 1))
        top = functools.reduce(jnp.maximum, levels)
        parts = [jnp.exp2(level - top) for level in levels]
        share = 1.0 / functools.reduce(jnp.add, parts)
        parts = [part * share for part in parts]
        for h in range(HEADS):
            cols = slice(h * HD, (h + 1) * HD)
            mixed = [came[j][:, cols].astype(F32) * parts[j][:, h : h + 1] for j in range(CTX)]
            heads[:, cols] = functools.reduce(jnp.add, mixed).astype(BF)

    @pl.when(meta[PREFILL] == 0)
    def _():
        load = pltpu.make_async_copy(pages, held, sems.at[0])
        load.start()
        for n in range(8):
            page = crossed.at[spots[64 + n]]
            pltpu.make_async_copy(page, relaid.at[spots[n]], sems.at[1]).start()
        for step in range(1, CTX):
            for n in range(8):
                relaid[spots[step * 8 + n]] = came[step][:, n * 2 * HD : (n + 1) * 2 * HD]
        for h in range(HEADS):
            q3[:, h, :] = mine[:, h * HD : (h + 1) * HD].astype(F32)
        load.wait()
        pltpu.make_async_copy(pages.at[pl.ds(0, 8)], relaid.at[pl.ds(0, 8)], sems.at[1]).wait()
        keep = pltpu.make_async_copy(relaid, pool, sems.at[2])
        keep.start()
        at_once = 8
        lane = lax.broadcasted_iota(jnp.int32, (HEADS, 2 * ROW), 1)

        def some(i, _):
            first = i * at_once
            own = mine[pl.ds(pl.multiple_of(first, at_once), at_once), HEADS * HD :].astype(F32)
            scores, own_scores, values = [], [], []
            for r in range(at_once):
                both = jnp.concatenate([held[first + r], relaid[first + r]], axis=0)
                queries = q3[first + r]
                s = lax.dot_general(queries.astype(BF), both[:, :HD], contract, preferred_element_type=F32)
                seen = (lane < lengths[first + r]) | (lane >= ROW)
                scores.append(jnp.where(seen, s, -1e30))
                own_scores.append(jnp.sum(queries * own[r : r + 1, :HD], axis=1, keepdims=True))
                values.append(both[:, HD:])
            scores = jnp.concatenate(scores, axis=0)
            own_scores = jnp.concatenate(own_scores, axis=0)
            top = jnp.maximum(jnp.max(scores, axis=1, keepdims=True), own_scores)
            weights = jnp.exp2((scores - top) * COEF)
            own_weights = jnp.exp2((own_scores - top) * COEF)
            total = jnp.sum(weights, axis=1, keepdims=True) + own_weights
            weights = weights.astype(BF)
            own_weights = own_weights.astype(BF).astype(F32)
            for r in range(at_once):
                rows = slice(r * HEADS, (r + 1) * HEADS)
                mixed = jnp.dot(weights[rows], values[r], preferred_element_type=F32)
                mixed = mixed + own_weights[rows] * own[r : r + 1, HD:]
                o3[first + r] = mixed / total[rows]
            return 0

        lax.fori_loop(0, ROW // at_once, some, 0)
        for h in range(HEADS):
            heads[:, h * HD : (h + 1) * HD] = o3[:, h, :].astype(BF)
        keep.wait()


def finish(meta, spots, lengths, mine, came, pages, crossed, pool):
    return pl.pallas_call(
        finish_kernel,
        in_specs=[SMEM] * 3 + [VMEM] * (1 + CTX) + [ANY] * 3,
        out_specs=[VMEM, ANY],
        out_shape=[
            jax.ShapeDtypeStruct((ROW, HEADS * HD), BF),
            jax.ShapeDtypeStruct(pool.shape, BF),
        ],
        scratch_shapes=[
            pltpu.VMEM(pool.shape, BF),
            pltpu.VMEM(pool.shape, BF),
            pltpu.VMEM((ROW, HEADS, HD), F32),
            pltpu.VMEM((ROW, HEADS, HD), F32),
            pltpu.SemaphoreType.DMA((3,)),
        ],
        input_output_aliases={6 + CTX: 1},
        compiler_params=params(),
        cost_estimate=pl.CostEstimate(flops=1 << 24, bytes_accessed=3 * nbytes(pool), transcendentals=1 << 16),
        name="finish",
    )(meta, spots, lengths, mine, *came, pages, crossed, pool)


def gather_rows(meta, chunks, rows, wanted):
    for s in range(CTX):
        origin = peer(meta[ME], STEPS[s], -1)
        sends = lax.bitwise_xor(origin, meta[TP]) & 1
        turn = (origin // 2 + 4 - meta[TP] // 2) % 4

        @pl.when(sends == wanted)
        def _():
            rows[pl.ds(pl.multiple_of(turn * ROW, ROW), ROW), :] = chunks[s][...]


def other_half_kernel(block, meta, *rest):
    chunks, w, out, rows = rest[:CTX], *rest[CTX:]
    gather_rows(meta, chunks, rows, 1)
    for n in range(0, w.shape[1], block):
        out[:, n : n + block] = jnp.dot(rows[...], w[:, n : n + block], preferred_element_type=F32)


def own_half_kernel(block, meta, *rest):
    chunks, w, out, rows = rest[:CTX], *rest[CTX:]
    gather_rows(meta, chunks, rows, 0)
    for n in range(0, w.shape[1], block):
        out[:, n : n + block] = jnp.dot(rows[...], w[:, n : n + block], preferred_element_type=F32)


def pair_kernel(own, came, *outs):
    for p in range(4):
        rows = slice(p * ROW, (p + 1) * ROW)
        outs[p][...] = (own[rows] + came[rows]).astype(outs[p].dtype)


def pair_sum(own, came):
    wide = own.shape[1]
    return pl.pallas_call(
        pair_kernel,
        in_specs=[VMEM] * 2,
        out_specs=[VMEM] * 4,
        out_shape=[jax.ShapeDtypeStruct((ROW, wide), F32 if p == 0 else BF) for p in range(4)],
        compiler_params=params(),
        cost_estimate=pl.CostEstimate(flops=1 << 19, bytes_accessed=nbytes(own, came), transcendentals=0),
        name="pair_sum",
    )(own, came)


def half(kernel, name, meta, chunks, w_out, block=512):
    depth, wide = w_out.shape
    return pl.pallas_call(
        functools.partial(kernel, block),
        in_specs=[SMEM] + [VMEM] * (CTX + 1),
        out_specs=VMEM,
        out_shape=jax.ShapeDtypeStruct((4 * ROW, wide), F32),
        scratch_shapes=[pltpu.VMEM((4 * ROW, depth), BF)],
        compiler_params=params(),
        cost_estimate=pl.CostEstimate(
            flops=8 * ROW * depth * wide, bytes_accessed=nbytes(w_out), transcendentals=0
        ),
        name=name,
    )(meta, *chunks, w_out)


def last_kernel(a, b, c, d, out):
    out[...] = (a[...] + b[...].astype(F32) + c[...].astype(F32) + d[...].astype(F32)).astype(BF)


def last_sum(parts):
    return pl.pallas_call(
        last_kernel,
        in_specs=[VMEM] * 4,
        out_specs=VMEM,
        out_shape=jax.ShapeDtypeStruct(parts[0].shape, BF),
        compiler_params=params(),
        cost_estimate=pl.CostEstimate(flops=1 << 19, bytes_accessed=nbytes(*parts), transcendentals=0),
        name="last_sum",
    )(*parts)


def shards(hidden_in, w_query, w_keyval, w_out, kv_pages, page_slot, lengths):
    meta = place_here()
    pages = kv_pages[0]
    flat_pages = pages.reshape(-1, pages.shape[2])

    def both_rings(value, s):
        return lax.ppermute(value, "ctx", [(c, peer(c, STEPS[s], 1)) for c in range(CTX)])

    def back(value, s):
        return lax.ppermute(value, "ctx", [(c, peer(c, STEPS[s], -1)) for c in range(CTX)])

    def across(value):
        pairs = [(c, CTX + (c ^ 4)) for c in range(CTX)]
        return lax.ppermute(value, ("group", "ctx"), pairs + [(b, a) for a, b in pairs])

    def swap(value):
        return lax.all_to_all(value, "ctx", 0, 0, tiled=True)

    crossed = across(pages)
    part = jnp.concatenate(
        [
            (jnp.dot(hidden_in[0], w, preferred_element_type=F32) * LIFT).astype(F16)
            for w in (w_query, w_keyval)
        ],
        axis=1,
    )
    came = swap(part.reshape(CTX, ROW, -1))
    mine = (jnp.sum(came.astype(F32), axis=0) * (1.0 / LIFT)).astype(BF)
    queries = mine[:, : HEADS * HD]
    spots = plan(meta, page_slot)
    groups = ((7, 6), (5, 4), (3, 2), (1,))
    asked = {s: both_rings(queries, s) for steps in groups for s in steps}
    *outs, pool = attend_first(groups[0], meta, flat_pages, mine, [asked[s] for s in groups[0]])
    outs = fill(groups[0], meta, spots, crossed, outs)
    came = {}
    before = []
    for n, steps in enumerate(groups):
        if n > 0:
            ask = [asked[s] for s in steps]
            outs = attend(steps, meta, spots, crossed, flat_pages, mine, ask, [outs[0]] + before)
            before = [came[s] for s in groups[n - 1]]
        for s, value in zip(steps, outs):
            came[s] = back(value, s)
    state = attend_own(meta, mine, flat_pages, outs[0])
    states = [state] + [came[s] for s in range(1, CTX)]
    heads, pool = finish(meta, spots, lengths, mine, states, pages, crossed, pool.reshape(pages.shape))
    gathered = [heads] + [both_rings(heads, s) for s in range(1, CTX)]
    sent = half(other_half_kernel, "other_half", meta, gathered, w_out)
    came = lax.ppermute(sent, "tp", [(t, t ^ 1) for t in range(8)])
    mine = pair_sum(half(own_half_kernel, "own_half", meta, gathered, w_out), came)
    totals = [mine[0]] + [
        lax.ppermute(mine[p], "tp", [(t, (t + 2 * p) % 8) for t in range(8)]) for p in range(1, 4)
    ]
    return (last_sum(totals)[None], pool[None])


def solution(mesh):
    placed = (
        P("group", None, "ctx"),
        P("ctx", "tp"),
        P("ctx", "tp"),
        P("tp", "ctx"),
        P("group", "ctx", None, "tp"),
        P(),
        P("ctx"),
    )
    return jax.shard_map(
        shards,
        mesh=mesh,
        in_specs=placed,
        out_specs=(P("group", "tp", "ctx"), P("group", "ctx", None, "tp")),
        check_vma=False,
    )
```

```python
import functools
import math

import jax
import jax.numpy as jnp
from jax import lax
from jax.experimental import pallas as pl
from jax.experimental.pallas import tpu as pltpu
from jax.sharding import PartitionSpec as P

HD = 128
HEADS = 8
STATE = (HEADS + 1) * HD
CTX = 8
ROW = 64
STEPS = ((0, 0), (1, 0), (0, 1), (0, 3), (1, 1), (1, 3), (0, 2), (1, 2))
COEF = HD ** -0.5 * math.log2(math.e)
BF = jnp.bfloat16
F32 = jnp.float32
F16 = jnp.float16
LIFT = 64.0
SMEM = pl.BlockSpec(memory_space=pltpu.SMEM)
VMEM = pl.BlockSpec(memory_space=pltpu.VMEM)
ANY = pl.BlockSpec(memory_space=pl.ANY)
PREFILL, ME, TP = 0, 1, 2


def peer(place, step, sign):
    flip, turn = step
    return (place // 4 ^ flip) * 4 + (place + sign * turn) % 4


def place_here():
    return jnp.stack([1 - lax.axis_index("group"), lax.axis_index("ctx"), lax.axis_index("tp")]).astype(jnp.int32)


def params(limit=24 << 20, **more):
    return pltpu.CompilerParams(vmem_limit_bytes=limit, **more)


def nbytes(*arrays):
    return sum(math.prod(a.shape) * a.dtype.itemsize for a in arrays)


def pages_for(slots, holder, target, found):
    origin = lax.bitwise_xor(holder, 4)

    def look(i, n):
        slot = slots[origin * 64 + i]
        there = lax.shift_right_logical(slot, 6) == target

        @pl.when(there)
        def _():
            found(n, i, lax.bitwise_and(slot, 63))

        return n + there.astype(jnp.int32)

    lax.fori_loop(0, 64, look, jnp.int32(0), unroll=4)


def places(meta, slots, spots):
    me = meta[ME]
    for step in range(CTX):
        def coming(n, page, slot):
            spots[step * 8 + n] = slot

        def leaving(n, page, slot):
            spots[64 + step * 8 + n] = page

        pages_for(slots, peer(me, STEPS[step], 1), me, coming)
        pages_for(slots, me, peer(me, STEPS[step], -1), leaving)


def weigh(pieces, state=None):
    new = functools.reduce(jnp.maximum, [jnp.max(scores, axis=1, keepdims=True) for scores, _ in pieces])
    l = acc = None
    if state is not None:
        m, l, acc = state
        new = jnp.maximum(m, new)
        fade = jnp.exp2((m - new) * COEF)
        l, acc = l * fade, acc * fade
    for scores, values in pieces:
        weights = jnp.exp2((scores - new) * COEF)
        lanes = [weights[:, x : x + HD] for x in range(0, weights.shape[1], HD)]
        lanes = functools.reduce(jnp.add, lanes)
        mixed = jnp.dot(weights.astype(BF), values, preferred_element_type=F32)
        l = lanes if l is None else l + lanes
        acc = mixed if acc is None else acc + mixed
    return (new, l, acc)


def attend_rows(meta, owner, block, q, kv, mine, out, q2, pair):
    contract = (((1,), (1,)), ((), ()))
    if q is not None:
        for h in range(HEADS):
            q2[h * ROW : (h + 1) * ROW, :] = q[:, h * HD : (h + 1) * HD]
    pair[:ROW, :] = mine[:, HEADS * HD :]
    pair[ROW:, :] = jnp.zeros((HD - ROW, 2 * HD), BF)
    ahead = (owner - meta[ME]) * ROW
    scores = lax.dot_general(q2[...], pair[:, :HD], contract, preferred_element_type=F32)
    token = lax.bitwise_and(lax.broadcasted_iota(jnp.int32, scores.shape, 0), ROW - 1)
    key = lax.broadcasted_iota(jnp.int32, scores.shape, 1)
    scores = jnp.where((key <= token + ahead) & (key < ROW), scores, -1e30)
    recent = (scores, pair[:, HD:])
    state = None
    for first in range(0, kv.shape[0], block):
        some = slice(first, first + block)
        scores = lax.dot_general(q2[...], kv[some, :HD], contract, preferred_element_type=F32)
        pieces = [(scores, kv[some, HD:])]
        state = weigh(pieces if state is not None else [recent] + pieces, state)
    m, l, acc = state
    l = jnp.sum(l, axis=1, keepdims=True)
    mixed = acc * (1.0 / l)
    level = m * COEF + jnp.log2(l)
    high = level.astype(BF).astype(F32)
    rest = level - high
    mid = rest.astype(BF).astype(F32)
    low = rest - mid
    lane = lax.broadcasted_iota(jnp.int32, (ROW, HD), 1)
    stats = jnp.zeros((ROW, HD), F32)
    for h in range(HEADS):
        rows = slice(h * ROW, (h + 1) * ROW)
        out[:, h * HD : (h + 1) * HD] = mixed[rows].astype(out.dtype)
        stats = jnp.where(lane == h, high[rows], stats)
        stats = jnp.where(lane == 8 + h, mid[rows], stats)
        stats = jnp.where(lane == 16 + h, low[rows], stats)
    out[:, HEADS * HD :] = stats.astype(out.dtype)


def own_kernel(block, meta, mine, kv, *rest):
    out, q2, pair = rest[-3:]
    @pl.when(meta[PREFILL] == 1)
    def _():
        attend_rows(meta, meta[ME], block, mine, kv, mine, out, q2, pair)


def attend_own(meta, mine, pages, after, block=2048):
    big = HEADS * ROW
    return pl.pallas_call(
        functools.partial(own_kernel, block),
        in_specs=[SMEM] + [VMEM] * 2 + [ANY] * len(after),
        out_specs=VMEM,
        out_shape=jax.ShapeDtypeStruct((ROW, STATE), F32),
        scratch_shapes=[pltpu.VMEM((big, HD), BF), pltpu.VMEM((HD, 2 * HD), BF)],
        compiler_params=params(),
        cost_estimate=pl.CostEstimate(flops=1 << 32, bytes_accessed=0, transcendentals=0),
        name="attend_own",
    )(meta, mine, pages, *after)


def attend_kernel(steps, block, meta, spots, crossed, kv, mine, *rest):
    queries, outs, (state, q2, pair, sem) = rest[: len(steps)], rest[-len(steps) - 4 : -4], rest[-4:]
    i = pl.program_id(0)

    @pl.when(meta[PREFILL] == 1)
    def _():
        attend_step(meta, steps, block, queries, kv, mine, outs, state, q2, pair)

    @pl.when((meta[PREFILL] == 0) & (i == 0))
    def _():
        fill_pages(steps, spots, crossed, outs, sem)


def attend_step(meta, steps, block, queries, kv, mine, outs, state, q2, pair):
    i = pl.program_id(0)
    owner = jnp.int32(0)
    for n, step in enumerate(steps):
        owner = jnp.where(i == n, peer(meta[ME], STEPS[step], -1), owner)
        @pl.when(i == n)
        def _():
            for h in range(HEADS):
                q2[h * ROW : (h + 1) * ROW, :] = queries[n][:, h * HD : (h + 1) * HD]
    attend_rows(meta, owner, block, None, kv, mine, state, q2, pair)
    for n in range(len(steps)):
        @pl.when(i == n)
        def _():
            outs[n][:, :STATE] = state[...]


def attend_scratch():
    return [
        pltpu.VMEM((ROW, STATE), BF),
        pltpu.VMEM((HEADS * ROW, HD), BF),
        pltpu.VMEM((HD, 2 * HD), BF),
    ]


def attend(steps, meta, spots, crossed, pages, mine, queries, after, block=2048):
    return pl.pallas_call(
        functools.partial(attend_kernel, steps, block),
        grid=(len(steps),),
        in_specs=[SMEM] * 2 + [ANY] + [VMEM] * (2 + len(queries)) + [ANY] * len(after),
        out_specs=[VMEM] * len(steps),
        out_shape=[jax.ShapeDtypeStruct((ROW, 16 * HD), BF)] * len(steps),
        scratch_shapes=attend_scratch() + [pltpu.SemaphoreType.DMA((len(steps), 8))],
        compiler_params=params(),
        cost_estimate=pl.CostEstimate(flops=len(steps) << 32, bytes_accessed=0, transcendentals=0),
        name=f"attend_{steps[0]}",
    )(meta, spots, crossed, pages, mine, *queries, *after)


def start_kernel(steps, block, meta, slots, kv, mine, *rest):
    queries, outs, (pool, spots, state, q2, pair, sem) = rest[: len(steps)], rest[-len(steps) - 6 : -6], rest[-6:]
    i = pl.program_id(0)

    @pl.when(meta[PREFILL] == 1)
    def _():
        keep = pltpu.make_async_copy(kv, pool, sem)

        @pl.when(i == 0)
        def _():
            keep.start()

        attend_step(meta, steps, block, queries, kv, mine, outs, state, q2, pair)

        @pl.when(i == len(steps) - 1)
        def _():
            keep.wait()

    @pl.when((meta[PREFILL] == 0) & (i == 0))
    def _():
        places(meta, slots, spots)


def attend_first(steps, meta, slots, pages, mine, queries, block=2048):
    return pl.pallas_call(
        functools.partial(start_kernel, steps, block),
        grid=(len(steps),),
        in_specs=[SMEM] * 2 + [VMEM] * (2 + len(queries)),
        out_specs=[VMEM] * len(steps) + [ANY, SMEM],
        out_shape=[jax.ShapeDtypeStruct((ROW, 16 * HD), BF)] * len(steps)
        + [jax.ShapeDtypeStruct(pages.shape, BF), jax.ShapeDtypeStruct((128,), jnp.int32)],
        scratch_shapes=attend_scratch() + [pltpu.SemaphoreType.DMA],
        compiler_params=params(),
        cost_estimate=pl.CostEstimate(flops=0, bytes_accessed=0, transcendentals=0),
        name=f"attend_{steps[0]}",
    )(meta, slots, pages, mine, *queries)


def fill_pages(steps, spots, crossed, outs, sem):
    copies = [
        pltpu.make_async_copy(
            crossed.at[spots[64 + step * 8 + p]], outs[n].at[:, p * 2 * HD : (p + 1) * 2 * HD], sem.at[n, p]
        )
        for n, step in enumerate(steps)
        for p in range(8)
    ]
    for copy in copies:
        copy.start()
    for copy in copies:
        copy.wait()


def fill_kernel(steps, meta, spots, crossed, *rest):
    outs, sem = rest[len(steps) : -1], rest[-1]

    @pl.when(meta[PREFILL] == 0)
    def _():
        fill_pages(steps, spots, crossed, outs, sem)


def fill(steps, meta, spots, crossed, values):
    return pl.pallas_call(
        functools.partial(fill_kernel, steps),
        in_specs=[SMEM] * 2 + [ANY] + [VMEM] * len(steps),
        out_specs=[VMEM] * len(steps),
        out_shape=[jax.ShapeDtypeStruct(value.shape, BF) for value in values],
        scratch_shapes=[pltpu.SemaphoreType.DMA((len(steps), 8))],
        input_output_aliases={3 + n: n for n in range(len(steps))},
        compiler_params=params(),
        cost_estimate=pl.CostEstimate(flops=0, bytes_accessed=0, transcendentals=0),
        name=f"fill_{steps[0]}",
    )(meta, spots, crossed, *values)


def finish_kernel(meta, spots, lengths, mine, *rest):
    came, (pages, crossed, _, heads, pool, held, relaid, q3, o3, own3, sems) = rest[:CTX], rest[CTX:]
    contract = (((1,), (1,)), ((), ()))

    @pl.when(meta[PREFILL] == 1)
    def _():
        levels = []
        for j in range(CTX):
            stats = came[j][:, HEADS * HD : STATE].astype(F32)
            levels.append(stats + pltpu.roll(stats, HD - 8, 1) + pltpu.roll(stats, HD - 16, 1))
        top = functools.reduce(jnp.maximum, levels)
        parts = [jnp.exp2(level - top) for level in levels]
        share = 1.0 / functools.reduce(jnp.add, parts)
        parts = [part * share for part in parts]
        for h in range(HEADS):
            cols = slice(h * HD, (h + 1) * HD)
            mixed = [came[j][:, cols].astype(F32) * parts[j][:, h : h + 1] for j in range(CTX)]
            heads[:, cols] = functools.reduce(jnp.add, mixed).astype(BF)

    @pl.when(meta[PREFILL] == 0)
    def _():
        load = pltpu.make_async_copy(pages, held, sems.at[0])
        load.start()
        for n in range(8):
            page = crossed.at[spots[64 + n]]
            pltpu.make_async_copy(page, relaid.at[spots[n]], sems.at[1]).start()
        for step in range(1, CTX):
            for n in range(8):
                relaid[spots[step * 8 + n]] = came[step][:, n * 2 * HD : (n + 1) * 2 * HD]
        for h in range(HEADS):
            q3[:, h, :] = mine[:, h * HD : (h + 1) * HD].astype(F32)
        own3[...] = mine[:, HEADS * HD :].astype(F32)
        load.wait()
        pltpu.make_async_copy(pages.at[pl.ds(0, 8)], relaid.at[pl.ds(0, 8)], sems.at[1]).wait()
        keep = pltpu.make_async_copy(relaid, pool, sems.at[2])
        keep.start()
        at_once = 8
        lane = lax.broadcasted_iota(jnp.int32, (HEADS, 2 * ROW), 1)

        def some(i, _):
            first = i * at_once
            own = own3[pl.ds(pl.multiple_of(first, at_once), at_once), :]
            scores, own_scores, values = [], [], []
            for r in range(at_once):
                both = jnp.concatenate([held[first + r], relaid[first + r]], axis=0)
                queries = q3[first + r]
                s = lax.dot_general(queries.astype(BF), both[:, :HD], contract, preferred_element_type=F32)
                seen = (lane < lengths[first + r]) | (lane >= ROW)
                scores.append(jnp.where(seen, s, -1e30))
                own_scores.append(jnp.sum(queries * own[r : r + 1, :HD], axis=1, keepdims=True))
                values.append(both[:, HD:])
            scores = jnp.concatenate(scores, axis=0)
            own_scores = jnp.concatenate(own_scores, axis=0)
            top = jnp.maximum(jnp.max(scores, axis=1, keepdims=True), own_scores)
            weights = jnp.exp2((scores - top) * COEF)
            own_weights = jnp.exp2((own_scores - top) * COEF)
            total = jnp.sum(weights, axis=1, keepdims=True) + own_weights
            own_weights = own_weights.astype(BF).astype(F32)
            for r in range(at_once):
                rows = slice(r * HEADS, (r + 1) * HEADS)
                mixed = jnp.dot(weights[rows].astype(BF), values[r], preferred_element_type=F32)
                mixed = mixed + own_weights[rows] * own[r : r + 1, HD:]
                o3[first + r] = mixed / total[rows]
            return 0

        lax.fori_loop(0, ROW // at_once, some, 0)
        for h in range(HEADS):
            heads[:, h * HD : (h + 1) * HD] = o3[:, h, :].astype(BF)
        keep.wait()


def finish(meta, spots, lengths, mine, came, pages, crossed, pool):
    return pl.pallas_call(
        finish_kernel,
        in_specs=[SMEM] * 3 + [VMEM] * (1 + CTX) + [ANY] * 3,
        out_specs=[VMEM, ANY],
        out_shape=[
            jax.ShapeDtypeStruct((ROW, HEADS * HD), BF),
            jax.ShapeDtypeStruct(pool.shape, BF),
        ],
        scratch_shapes=[
            pltpu.VMEM(pool.shape, BF),
            pltpu.VMEM(pool.shape, BF),
            pltpu.VMEM((ROW, HEADS, HD), F32),
            pltpu.VMEM((ROW, HEADS, HD), F32),
            pltpu.VMEM((ROW, 2 * HD), F32),
            pltpu.SemaphoreType.DMA((3,)),
        ],
        input_output_aliases={6 + CTX: 1},
        compiler_params=params(),
        cost_estimate=pl.CostEstimate(flops=1 << 24, bytes_accessed=3 * nbytes(pool), transcendentals=1 << 16),
        name="finish",
    )(meta, spots, lengths, mine, *came, pages, crossed, pool)


def gather_rows(meta, chunks, rows, wanted):
    for s in range(CTX):
        origin = peer(meta[ME], STEPS[s], -1)
        sends = lax.bitwise_xor(origin, meta[TP]) & 1
        turn = (origin // 2 + 4 - meta[TP] // 2) % 4

        @pl.when(sends == wanted)
        def _():
            rows[pl.ds(pl.multiple_of(turn * ROW, ROW), ROW), :] = chunks[s][...]


def other_half_kernel(block, meta, *rest):
    chunks, w, out, rows = rest[:CTX], *rest[CTX:]
    gather_rows(meta, chunks, rows, 1)
    for n in range(0, w.shape[1], block):
        out[:, n : n + block] = jnp.dot(rows[...], w[:, n : n + block], preferred_element_type=F32)


def own_half_kernel(block, meta, *rest):
    chunks, w, out, rows = rest[:CTX], *rest[CTX:]
    gather_rows(meta, chunks, rows, 0)
    for n in range(0, w.shape[1], block):
        out[:, n : n + block] = jnp.dot(rows[...], w[:, n : n + block], preferred_element_type=F32)


def pair_kernel(own, came, *outs):
    for p in range(4):
        rows = slice(p * ROW, (p + 1) * ROW)
        outs[p][...] = (own[rows] + came[rows]).astype(outs[p].dtype)


def pair_sum(own, came):
    wide = own.shape[1]
    return pl.pallas_call(
        pair_kernel,
        in_specs=[VMEM] * 2,
        out_specs=[VMEM] * 4,
        out_shape=[jax.ShapeDtypeStruct((ROW, wide), F32 if p == 0 else BF) for p in range(4)],
        compiler_params=params(),
        cost_estimate=pl.CostEstimate(flops=1 << 19, bytes_accessed=nbytes(own, came), transcendentals=0),
        name="pair_sum",
    )(own, came)


def half(kernel, name, meta, chunks, w_out, block=512):
    depth, wide = w_out.shape
    return pl.pallas_call(
        functools.partial(kernel, block),
        in_specs=[SMEM] + [VMEM] * (CTX + 1),
        out_specs=VMEM,
        out_shape=jax.ShapeDtypeStruct((4 * ROW, wide), F32),
        scratch_shapes=[pltpu.VMEM((4 * ROW, depth), BF)],
        compiler_params=params(),
        cost_estimate=pl.CostEstimate(
            flops=8 * ROW * depth * wide, bytes_accessed=nbytes(w_out), transcendentals=0
        ),
        name=name,
    )(meta, *chunks, w_out)


def last_kernel(a, b, c, d, out):
    out[...] = (a[...] + b[...].astype(F32) + c[...].astype(F32) + d[...].astype(F32)).astype(BF)


def last_sum(parts):
    return pl.pallas_call(
        last_kernel,
        in_specs=[VMEM] * 4,
        out_specs=VMEM,
        out_shape=jax.ShapeDtypeStruct(parts[0].shape, BF),
        compiler_params=params(),
        cost_estimate=pl.CostEstimate(flops=1 << 19, bytes_accessed=nbytes(*parts), transcendentals=0),
        name="last_sum",
    )(*parts)


def shards(hidden_in, w_query, w_keyval, w_out, kv_pages, page_slot, lengths):
    meta = place_here()
    pages = kv_pages[0]
    flat_pages = pages.reshape(-1, pages.shape[2])

    def both_rings(value, s):
        return lax.ppermute(value, "ctx", [(c, peer(c, STEPS[s], 1)) for c in range(CTX)])

    def back(value, s):
        return lax.ppermute(value, "ctx", [(c, peer(c, STEPS[s], -1)) for c in range(CTX)])

    def across(value):
        pairs = [(c, CTX + (c ^ 4)) for c in range(CTX)]
        return lax.ppermute(value, ("group", "ctx"), pairs + [(b, a) for a, b in pairs])

    def swap(value):
        return lax.all_to_all(value, "ctx", 0, 0, tiled=True)

    crossed = across(pages)
    part = jnp.concatenate(
        [
            (jnp.dot(hidden_in[0], w, preferred_element_type=F32) * LIFT).astype(F16)
            for w in (w_query, w_keyval)
        ],
        axis=1,
    )
    came = swap(part.reshape(CTX, ROW, -1))
    mine = (jnp.sum(came.astype(F32), axis=0) * (1.0 / LIFT)).astype(BF)
    queries = mine[:, : HEADS * HD]
    groups = ((7, 6), (5, 4), (3, 2), (1,))
    asked = {s: both_rings(queries, s) for steps in groups for s in steps}
    *outs, pool, spots = attend_first(groups[0], meta, page_slot, flat_pages, mine, [asked[s] for s in groups[0]])
    outs = fill(groups[0], meta, spots, crossed, outs)
    came = {}
    before = []
    for n, steps in enumerate(groups):
        if n > 0:
            ask = [asked[s] for s in steps]
            outs = attend(steps, meta, spots, crossed, flat_pages, mine, ask, [outs[0]] + before)
            before = [came[s] for s in groups[n - 1]]
        for s, value in zip(steps, outs):
            came[s] = back(value, s)
    state = attend_own(meta, mine, flat_pages, [outs[0]] + before)
    states = [state] + [came[s] for s in range(1, CTX)]
    heads, pool = finish(meta, spots, lengths, mine, states, pages, crossed, pool.reshape(pages.shape))
    gathered = [heads] + [both_rings(heads, s) for s in range(1, CTX)]
    sent = half(other_half_kernel, "other_half", meta, gathered, w_out)
    came = lax.ppermute(sent, "tp", [(t, t ^ 1) for t in range(8)])
    mine = pair_sum(half(own_half_kernel, "own_half", meta, gathered, w_out), came)
    totals = [mine[0]] + [
        lax.ppermute(mine[p], "tp", [(t, (t + 2 * p) % 8) for t in range(8)]) for p in range(1, 4)
    ]
    return (last_sum(totals)[None], pool[None])


def solution(mesh):
    placed = (
        P("group", None, "ctx"),
        P("ctx", "tp"),
        P("ctx", "tp"),
        P("tp", "ctx"),
        P("group", "ctx", None, "tp"),
        P(),
        P("ctx"),
    )
    return jax.shard_map(
        shards,
        mesh=mesh,
        in_specs=placed,
        out_specs=(P("group", "tp", "ctx"), P("group", "ctx", None, "tp")),
        check_vma=False,
    )
```
